128 devices in a mesh: tm: 4 (over y), height: 8 (over x_lo, z), seq: 4 (over x_hi, core).
Axes of the slice: x: 4 (x_hi: 2, x_lo: 2; x = x_hi * 2 + x_lo), y: 4, z: 4, core: 2. Of those that a mesh axis runs over, the one named last changes fastest.
Arguments:
- latents: float32 [1, 16, 16, 32, 64], P(None, 'tm', None, ('height', 'seq')), may hold values from -8 to 8
- w_in: float32 [3, 3, 3, 16, 384], replicated, may hold values from -0.3125 to 0.3125
- b_in: float32 [384], replicated, may hold values from -1.8 to 1.8
- norm_gain: float32 [384], replicated, may hold values from 0.1 to 1.9
- norm_shift: float32 [384], replicated, may hold values from -1.8 to 1.8
- w_mid: float32 [3, 3, 3, 384, 384], replicated, may hold values from -0.0625 to 0.0625
- b_mid: float32 [384], replicated, may hold values from -1.8 to 1.8
- w_time: float32 [3, 384, 768], replicated, may hold values from -0.1875 to 0.1875
- b_time: float32 [768], replicated, may hold values from -1.8 to 1.8
- w_up: float32 [3, 3, 384, 192], replicated, may hold values from -0.109375 to 0.109375
- b_up: float32 [192], replicated, may hold values from -1.8 to 1.8
Outputs:
- decoded: float32 [1, 32, 64, 128, 192], P(None, ('tm', 'seq'), 'height')
The draws below stay inside these ranges and needn't reach their ends.
All inputs are finite; a program needn't handle non-finite values.
Results may differ from the reference program's by a relative error of at most 0.0001.
Values sent between devices are 32-bit elements; how exact they have to be, the bound alone decides.
No kernel may reach another device: no remote copies, remote signals or barrier semaphores. Data moves between devices by JAX's collectives and lax.ppermute only.
A program may use at most 128 MiB of HBM per device.

```python
import jax
import jax.numpy as jnp
from jax import lax

CHANNELS = 384
LATENT = 16
COLS = 64
CLIPS = 1
FRAMES = 16
ROWS = 32
UP_CH = 192


def draw_latents(key, part):
    key = jax.random.fold_in(key, 17)
    normal_key, rough_key = jax.random.split(key)
    full_shape = (CLIPS, FRAMES, LATENT, ROWS, COLS)
    row_place = jnp.arange(ROWS, dtype=jnp.float32) / max(ROWS - 1, 1)
    row_scale = (0.6 * jnp.exp(jnp.log(3.0) * row_place))[None, None, None, :, None]
    roughness = jnp.exp(jax.random.uniform(rough_key, full_shape, jnp.float32, -0.35, 0.35))
    values_out = jax.random.normal(normal_key, full_shape, jnp.float32) * roughness * row_scale
    return jnp.clip(values_out, -8.0, 8.0)


def scatter_about(own_key, extent, width, reach, kind=jnp.bfloat16):
    return jnp.clip(width * jax.random.normal(own_key, extent, jnp.float32), -reach, reach).astype(kind)


def setup_inputs(seed: int = 0) -> dict:
    key_of = jax.random.split(jax.random.key(seed), 12)
    return {
        "latents": draw_latents(jax.random.fold_in(key_of[11], 71), 0),
        "w_in": scatter_about(key_of[1], (3, 3, 3, LATENT, CHANNELS), (27 * LATENT) ** -0.5, 0.3125, jnp.float32),
        "b_in": scatter_about(key_of[2], (CHANNELS,), 0.3, 1.8, jnp.float32),
        "norm_gain": jnp.clip(1.0 + 0.18 * jax.random.normal(key_of[3], (CHANNELS,), jnp.float32), 0.1, 1.9),
        "norm_shift": scatter_about(key_of[4], (CHANNELS,), 0.3, 1.8, jnp.float32),
        "w_mid": scatter_about(key_of[5], (3, 3, 3, CHANNELS, CHANNELS), (27 * CHANNELS) ** -0.5, 0.0625, jnp.float32),
        "b_mid": scatter_about(key_of[6], (CHANNELS,), 0.3, 1.8, jnp.float32),
        "w_time": scatter_about(key_of[7], (3, CHANNELS, 2 * CHANNELS), (3 * CHANNELS) ** -0.5, 0.1875, jnp.float32),
        "b_time": scatter_about(key_of[8], (2 * CHANNELS,), 0.3, 1.8, jnp.float32),
        "w_up": scatter_about(key_of[9], (3, 3, CHANNELS, UP_CH), (9 * CHANNELS) ** -0.5, 0.109375, jnp.float32),
        "b_up": scatter_about(key_of[10], (UP_CH,), 0.3, 1.8, jnp.float32),
    }


epsilon = 1e-06
exact_mode = lax.Precision.HIGHEST

def double(tensor, along):
    stacked = jnp.stack([tensor, tensor], axis=along + 1)
    new_shape = list(tensor.shape)
    new_shape[along] = 2 * new_shape[along]
    return stacked.reshape(new_shape)

def causal_conv(tensor, weight, offset):
    n_clips, n_frames, n_rows, n_cols, n_chan = tensor.shape
    padded = jnp.pad(tensor, ((0, 0), (2, 0), (1, 1), (1, 1), (0, 0)))
    summed = jnp.zeros((n_clips * n_frames * n_rows * n_cols, weight.shape[-1]), jnp.float32)
    for back_step in range(3):
        for down_step in range(3):
            for side_step in range(3):
                window = padded[:, back_step:back_step + n_frames, down_step:down_step + n_rows, side_step:side_step + n_cols]
                summed = summed + jnp.dot(window.reshape(-1, n_chan), weight[back_step, down_step, side_step], precision=exact_mode, preferred_element_type=jnp.float32)
    return (summed + offset).reshape(n_clips, n_frames, n_rows, n_cols, -1)

def rms_norm(tensor, scale_vec, shift_vec):
    mean_square = lax.optimization_barrier(jnp.mean(tensor * tensor, axis=-1, keepdims=True))
    normed = tensor / jnp.sqrt(mean_square + epsilon)
    return jax.nn.silu(normed * scale_vec + shift_vec)

def reference(latents, w_in, b_in, norm_gain, norm_shift, w_mid, b_mid, w_time, b_time, w_up, b_up):
    channels_last = jnp.transpose(latents, (0, 1, 3, 4, 2))
    initial = causal_conv(channels_last, w_in, b_in)
    hidden = rms_norm(initial, norm_gain, norm_shift)
    blended = initial + causal_conv(hidden, w_mid, b_mid)
    n_clips, n_frames, n_rows, n_cols, n_chan = blended.shape
    padded = jnp.pad(blended, ((0, 0), (2, 0), (0, 0), (0, 0), (0, 0)))
    summed = jnp.zeros((n_clips * n_frames * n_rows * n_cols, 2 * n_chan), jnp.float32)
    for back_step in range(3):
        window = padded[:, back_step:back_step + n_frames].reshape(-1, n_chan)
        summed = summed + jnp.dot(window, w_time[back_step], precision=exact_mode, preferred_element_type=jnp.float32)
    paired = (summed + b_time).reshape(n_clips, n_frames, n_rows, n_cols, 2, n_chan)
    doubled = jnp.transpose(paired, (0, 1, 4, 2, 3, 5)).reshape(n_clips * 2 * n_frames, n_rows, n_cols, n_chan)

    def upsample_frame(image):
        widened = double(double(image, 0), 1)
        padded_img = jnp.pad(widened, ((1, 1), (1, 1), (0, 0)))
        summed_img = jnp.zeros((4 * n_rows * n_cols, w_up.shape[-1]), jnp.float32)
        for down_step in range(3):
            for side_step in range(3):
                window = padded_img[down_step:down_step + 2 * n_rows, side_step:side_step + 2 * n_cols].reshape(-1, n_chan)
                summed_img = summed_img + jnp.dot(window, w_up[down_step, side_step], precision=exact_mode, preferred_element_type=jnp.float32)
        return (summed_img + b_up).reshape(2 * n_rows, 2 * n_cols, -1)
    decoded = lax.map(upsample_frame, doubled)
    return decoded.reshape(n_clips, 2 * n_frames, 2 * n_rows, 2 * n_cols, -1)
```

```python
import jax
import jax.numpy as jnp
from jax import lax
from jax.experimental import pallas as pl
from jax.experimental.pallas import tpu as pltpu
from jax.sharding import PartitionSpec as P

EPS = 1e-06
F32 = jnp.float32
BF16 = jnp.bfloat16
AXES = ("tm", "height", "seq")
VMEM = pl.BlockSpec(memory_space=pltpu.VMEM)
ANY = pl.BlockSpec(memory_space=pl.ANY)


def split(value):
    hi = value.astype(BF16)
    return hi, (value - hi.astype(F32)).astype(BF16)


def dot(a, b):
    return jnp.dot(a, b, preferred_element_type=F32)


def dot_rows(a, b):
    return lax.dot_general(a, b, (((0,), (0,)), ((), ())), preferred_element_type=F32)


def send(value, target):
    n_tm, n_height, n_seq = (lax.axis_size(axis) for axis in AXES)
    place = lambda t, h, s: (t * n_height + h) * n_seq + s
    pairs = []
    for t in range(n_tm):
        for h in range(n_height):
            for s in range(n_seq):
                end = target(t, h, s)
                if end is not None and 0 <= end[0] < n_tm and 0 <= end[1] < n_height:
                    pairs.append((place(t, h, s), place(*end)))
    return lax.ppermute(value, AXES, pairs)


def blend_kernel(
    up_ref, mid_ref, down_ref, w_in_ref, b_in_ref, gain_ref, shift_ref, b_mid_ref, w_mid_ref,
    own_ref, send_ref,
    raw, taps_hi, taps_lo, start, inner_hi, inner_lo, w_hi, w_lo, acc, sems,
):
    for slot, lag in enumerate((0, 2, 1)):
        pltpu.make_async_copy(w_mid_ref.at[lag], raw.at[lag], sems.at[lag]).start()

    t, h, s = (lax.axis_index(axis) for axis in AXES)
    core = lax.rem(s, 2)
    first = 4 * t + 2 * lax.div(s, 2) + 2 * core - 4

    lat = jnp.concatenate(
        [ref[j] for ref in (up_ref, mid_ref, down_ref) for j in range(2)], axis=1
    )
    col = lax.broadcasted_iota(jnp.int32, (1, 512), 1) % 64
    for down in range(3):
        for side in range(3):
            offset = 64 * (1 + down) + side - 1
            piece = pltpu.roll(lat, 768 - offset, 1)[:, :512]
            if side == 0:
                piece = jnp.where(col == 0, 0.0, piece)
            if side == 2:
                piece = jnp.where(col == 63, 0.0, piece)
            hi, lo = split(piece)
            for f in range(6):
                at = f * 144 + (down * 3 + side) * 16
                taps_hi[at : at + 16, :] = hi[f * 16 : f * 16 + 16]
                taps_lo[at : at + 16, :] = lo[f * 16 : f * 16 + 16]

    win_hi, win_lo = split(w_in_ref[...])
    row = lax.broadcasted_iota(jnp.int32, (512, 1), 0) // 64 + (4 * h - 2)
    row_ok = jnp.logical_and(row >= 0, row < 32)
    hidden = []
    for f in range(4):
        x_hi = taps_hi[f * 144 : f * 144 + 432, :]
        x_lo = taps_lo[f * 144 : f * 144 + 432, :]
        init = dot_rows(x_hi, win_hi) + dot_rows(x_lo, win_hi) + dot_rows(x_hi, win_lo)
        init = init + b_in_ref[...]
        if f >= 2:
            start[f - 2] = init[64:448]
        mean_square = jnp.mean(init * init, axis=-1, keepdims=True)
        value = init / jnp.sqrt(mean_square + EPS) * gain_ref[...] + shift_ref[...]
        value = value / (1.0 + jnp.exp(-value))
        hidden.append(jnp.where(jnp.logical_and(row_ok, first + f >= 0), value, 0.0))

    d0, d1, d2, d3 = hidden
    for p, value in enumerate((d0 - d2, d1 - d3, d1 + d2, d2 - d1)):
        hi, lo = split(value)
        for down in range(3):
            inner_hi[p, :, down * 384 : down * 384 + 384] = hi[down * 64 : down * 64 + 384]
            inner_lo[p, :, down * 384 : down * 384 + 384] = lo[down * 64 : down * 64 + 384]

    for p in range(4):
        if p < 3:
            lag = (0, 2, 1)[p]
            pltpu.make_async_copy(w_mid_ref.at[lag], raw.at[lag], sems.at[lag]).wait()
        for down in range(3):
            for side in range(3):
                if p == 0:
                    w = raw[0, down, side]
                elif p == 1:
                    w = raw[2, down, side]
                else:
                    even = 0.5 * (raw[0, down, side] + raw[2, down, side])
                    odd = 0.5 * raw[1, down, side]
                    w = even + odd if p == 2 else even - odd
                hi, lo = split(w)
                at = (p % 2, slice(down * 384, down * 384 + 384), slice(side * 384, side * 384 + 384))
                w_hi[at] = hi
                w_lo[at] = lo
        b_hi, b_lo = w_hi[p % 2], w_lo[p % 2]
        y = dot(inner_hi[p], b_hi) + dot(inner_lo[p], b_hi) + dot(inner_hi[p], b_lo)
        if p == 0:
            acc[0] = y
        elif p == 1:
            acc[1] = -y
        elif p == 2:
            acc[0] += y
            acc[1] += y
        else:
            acc[0] += y
            acc[1] -= y

    place = lax.broadcasted_iota(jnp.int32, (384, 1), 0) % 64
    for j in range(2):
        left = jnp.where(place == 0, 0.0, pltpu.roll(acc[j, :, 0:384], 1, 0))
        right = jnp.where(place == 63, 0.0, pltpu.roll(acc[j, :, 768:1152], 383, 0))
        out = start[j] + b_mid_ref[...] + left + acc[j, :, 384:768] + right
        own_ref[j] = jnp.where(first + 2 + j >= 0, out, 0.0)
    send_ref[...] = own_ref[1 - core]


def upsample_kernel(
    own_ref, got_ref, w_time_ref, b_time_ref, w_up_ref, b_up_ref,
    out_ref,
    hist_hi, hist_lo, x_hi, x_lo, d_hi, d_lo, mixed,
):
    h, s = lax.axis_index("height"), lax.axis_index("seq")
    even_core = lax.rem(s, 2) == 0
    own0, own1, got = own_ref[0], own_ref[1], got_ref[...]
    frames = (
        jnp.where(even_core, own0, got),
        jnp.where(even_core, own1, own0),
        jnp.where(even_core, got, own1),
    )
    for lag, value in enumerate(frames):
        hist_hi[:, lag * 384 : lag * 384 + 384], hist_lo[:, lag * 384 : lag * 384 + 384] = split(value)
    t_hi, t_lo = split(w_time_ref[...])
    paired = dot(hist_hi[...], t_hi) + dot(hist_lo[...], t_hi) + dot(hist_hi[...], t_lo)
    row = lax.broadcasted_iota(jnp.int32, (384, 1), 0) // 64 + (4 * h - 1)
    paired = jnp.where(jnp.logical_and(row >= 0, row < 32), paired + b_time_ref[...], 0.0)

    place = lax.broadcasted_iota(jnp.int32, (384, 1), 0) % 64
    for f in range(2):
        x = paired[:, f * 384 : f * 384 + 384]
        left = jnp.where(place == 0, 0.0, pltpu.roll(x, 1, 0))
        right = jnp.where(place == 63, 0.0, pltpu.roll(x, 383, 0))
        for c, value in enumerate((left, x, right)):
            lanes = slice(c * 384, c * 384 + 384)
            x_hi[f, :, lanes], x_lo[f, :, lanes] = split(value[64:320])
            d_hi[f, :, lanes], d_lo[f, :, lanes] = split(value[0:320] - value[64:384])

    b_up = jnp.concatenate([b_up_ref[...], jnp.zeros((1, 64), F32)], axis=1)
    for b in range(2):
        weights = []
        for sel in ((0,), (0, 1, 2), (2,)):
            cols = [sum(w_up_ref[r, c] for r in sel) for c in range(3)]
            parts = (cols[0], cols[1] + cols[2]) if b == 0 else (cols[0] + cols[1], cols[2])
            both = jnp.concatenate(parts, axis=0)
            weights.append(split(jnp.concatenate([both, jnp.zeros((768, 64), F32)], axis=1)))
        lanes = slice(b * 384, b * 384 + 768)
        for f in range(2):
            def product(hi, lo, w):
                return dot(hi, w[0]) + dot(lo, w[0]) + dot(hi, w[1])

            m1 = product(d_hi[f, 0:256, lanes], d_lo[f, 0:256, lanes], weights[0])
            m2 = product(x_hi[f, :, lanes], x_lo[f, :, lanes], weights[1]) + b_up
            m3 = product(d_hi[f, 64:320, lanes], d_lo[f, 64:320, lanes], weights[2])
            for a, value in enumerate((m1 + m2, m2 - m3)):
                for i in range(4):
                    for j in range(2):
                        mixed[f, 2 * i + a, j, pl.ds(b, 64, stride=2), :] = value[
                            i * 64 : i * 64 + 64, j * 128 : j * 128 + 128
                        ]
    out_ref[:, :, :, 0:128] = mixed[:, :, 0]
    out_ref[:, :, :, 128:192] = mixed[:, :, 1, :, 0:64]


def gather_latents(latents):
    s = lax.axis_index("seq")
    core, half = s % 2, s // 2
    row = latents[0, :, :, 0, :]
    other = send(row, lambda t, h, s: (t, h, s ^ 1))
    pair = jnp.where(
        core == 0, jnp.concatenate([row, other], axis=-1), jnp.concatenate([other, row], axis=-1)
    )
    other = send(pair, lambda t, h, s: (t, h, s ^ 2))
    slab = jnp.where(half == 0, jnp.stack([pair, other]), jnp.stack([other, pair]))
    before = send(slab, lambda t, h, s: (t + 2 if s == 0 else t + 1, h, s))
    beside = send(before, lambda t, h, s: (t, h, 0) if s == 1 else None)
    frames = jnp.where(
        s == 0,
        jnp.concatenate([before[:, 2:], beside], axis=1),
        jnp.where(
            s == 3,
            jnp.concatenate([before[:, 2:], slab], axis=1),
            jnp.concatenate([before, slab[:, :2]], axis=1),
        ),
    ).reshape(2, 96, 128)
    up = send(frames, lambda t, h, s: (t, h + 1, s))
    down = send(frames, lambda t, h, s: (t, h - 1, s))
    return up, frames, down


def body(latents, w_in, b_in, norm_gain, norm_shift, w_mid, b_mid, w_time, b_time, w_up, b_up):
    up, frames, down = gather_latents(latents)
    own, outgoing = pl.pallas_call(
        blend_kernel,
        out_shape=(
            jax.ShapeDtypeStruct((2, 384, 384), F32),
            jax.ShapeDtypeStruct((384, 384), F32),
        ),
        in_specs=[VMEM] * 8 + [ANY],
        out_specs=(VMEM, VMEM),
        scratch_shapes=[
            pltpu.VMEM((3, 3, 3, 384, 384), F32),
            pltpu.VMEM((864, 512), BF16),
            pltpu.VMEM((864, 512), BF16),
            pltpu.VMEM((2, 384, 384), F32),
            pltpu.VMEM((4, 384, 1152), BF16),
            pltpu.VMEM((4, 384, 1152), BF16),
            pltpu.VMEM((2, 1152, 1152), BF16),
            pltpu.VMEM((2, 1152, 1152), BF16),
            pltpu.VMEM((2, 384, 1152), F32),
            pltpu.SemaphoreType.DMA((3,)),
        ],
        compiler_params=pltpu.CompilerParams(vmem_limit_bytes=60 << 20),
        name="blend",
    )(
        up, frames, down, w_in.reshape(432, 384), b_in[None], norm_gain[None], norm_shift[None],
        b_mid[None], w_mid,
    )
    got = send(outgoing, lambda t, h, s: (t, h, s ^ 1))
    out = pl.pallas_call(
        upsample_kernel,
        out_shape=jax.ShapeDtypeStruct((2, 8, 128, 192), F32),
        in_specs=[VMEM] * 6,
        out_specs=VMEM,
        scratch_shapes=[
            pltpu.VMEM((384, 1152), BF16),
            pltpu.VMEM((384, 1152), BF16),
            pltpu.VMEM((2, 256, 1152), BF16),
            pltpu.VMEM((2, 256, 1152), BF16),
            pltpu.VMEM((2, 320, 1152), BF16),
            pltpu.VMEM((2, 320, 1152), BF16),
            pltpu.VMEM((2, 8, 2, 128, 128), F32),
        ],
        compiler_params=pltpu.CompilerParams(vmem_limit_bytes=60 << 20),
        name="upsample",
    )(own, got, w_time.reshape(1152, 768), b_time[None], w_up, b_up[None])
    return out[None]


def solution(mesh):
    placed = (P(None, "tm", None, ("height", "seq"), None),) + (P(),) * 10
    return jax.shard_map(
        body,
        mesh=mesh,
        in_specs=placed,
        out_specs=P(None, ("tm", "seq"), "height", None, None),
        check_vma=False,
    )
```

```python
import jax
import jax.numpy as jnp
from jax import lax
from jax.experimental import pallas as pl
from jax.experimental.pallas import tpu as pltpu
from jax.sharding import PartitionSpec as P

EPS = 1e-06
F32 = jnp.float32
BF16 = jnp.bfloat16
AXES = ("tm", "height", "seq")
COST = 10_000_000_000
VMEM = pl.BlockSpec(memory_space=pltpu.VMEM)


def dot_lanes(a, b):
    return lax.dot_general(a, b, (((1,), (1,)), ((), ())), preferred_element_type=F32)


def split(value):
    hi = value.astype(BF16)
    return hi, (value - hi.astype(F32)).astype(BF16)


def dot(a, b):
    return jnp.dot(a, b, preferred_element_type=F32)


def dot_rows(a, b):
    return lax.dot_general(a, b, (((0,), (0,)), ((), ())), preferred_element_type=F32)


def send(value, target):
    n_tm, n_height, n_seq = (lax.axis_size(axis) for axis in AXES)
    place = lambda t, h, s: (t * n_height + h) * n_seq + s
    pairs = []
    for t in range(n_tm):
        for h in range(n_height):
            for s in range(n_seq):
                end = target(t, h, s)
                if end is not None and 0 <= end[0] < n_tm and 0 <= end[1] < n_height:
                    pairs.append((place(t, h, s), place(*end)))
    return lax.ppermute(value, AXES, pairs)


def blend_kernel(
    mid_ref, far_ref, near_ref, w_in_ref, b_in_ref, gain_ref, shift_ref, b_mid_ref, raw,
    own_ref, send_ref,
    taps_hi, taps_lo, start, inner, weights, acc,
):
    t, h, s = (lax.axis_index(axis) for axis in AXES)
    core = lax.rem(s, 2)
    first = 4 * t + 2 * lax.div(s, 2) + 2 * core - 4

    mine, far, near = (
        [ref[j, pl.ds(pl.multiple_of(core * 32, 32), 96), :] for j in range(2)]
        for ref in (mid_ref, far_ref, near_ref)
    )
    up = [jnp.where(core == 0, a, b) for a, b in zip(far, near)]
    down = [jnp.where(core == 0, b, a) for a, b in zip(far, near)]
    lat = jnp.concatenate(up + mine + down, axis=1)
    col = lax.broadcasted_iota(jnp.int32, (1, 512), 1) % 64
    for down in range(3):
        for side in range(3):
            offset = 64 * (1 + down) + side - 1
            piece = pltpu.roll(lat, 768 - offset, 1)[:, :512]
            if side == 0:
                piece = jnp.where(col == 0, 0.0, piece)
            if side == 2:
                piece = jnp.where(col == 63, 0.0, piece)
            hi, lo = split(piece)
            for f in range(6):
                at = f * 144 + (down * 3 + side) * 16
                taps_hi[at : at + 16, :] = hi[f * 16 : f * 16 + 16]
                taps_lo[at : at + 16, :] = lo[f * 16 : f * 16 + 16]

    def fill(p, part):
        for unit in range(9 * part, 9 * part + 9):
            side, rows = unit // 12, slice(unit % 12 * 32, unit % 12 * 32 + 32)
            lanes = slice(side * 384, side * 384 + 384)
            lags = []
            for down in range(3):
                if p < 2:
                    lags.append(raw[2 * p, down, side, rows, :])
                else:
                    even = raw[0, down, side, rows, :] + raw[2, down, side, rows, :]
                    odd = raw[1, down, side, rows, :]
                    lags.append(even + odd if p == 2 else even - odd)
            even = lags[0] + lags[2]
            for q, w in enumerate((lags[0], lags[2], even + lags[1], even - lags[1])):
                hi, lo = split(w)
                weights[p % 2, q, rows, lanes] = hi
                weights[p % 2, q, slice(rows.start + 384, rows.stop + 384), lanes] = lo

    b_in, gain, shift, b_mid = (ref[...][None] for ref in (b_in_ref, gain_ref, shift_ref, b_mid_ref))
    win_hi, win_lo = split(w_in_ref[...])
    row = lax.broadcasted_iota(jnp.int32, (512, 1), 0) // 64 + (4 * h - 2)
    row_ok = jnp.logical_and(row >= 0, row < 32)
    hidden = []
    for f in range(4):
        x_hi = taps_hi[f * 144 : f * 144 + 432, :]
        x_lo = taps_lo[f * 144 : f * 144 + 432, :]
        init = dot_rows(x_hi, win_hi) + dot_rows(x_lo, win_hi) + dot_rows(x_hi, win_lo)
        init = init + b_in
        if f >= 2:
            start[f - 2] = init[64:448]
        mean_square = jnp.mean(init * init, axis=-1, keepdims=True)
        value = init / jnp.sqrt(mean_square + EPS) * gain + shift
        value = value / (1.0 + jnp.exp(-value))
        hidden.append(jnp.where(jnp.logical_and(row_ok, first + f >= 0), value, 0.0))
        fill(0, f)

    d0, d1, d2, d3 = hidden
    for p, value in enumerate((d0 - d2, d1 - d3, 0.5 * (d1 + d2), 0.5 * (d2 - d1))):
        for i in range(3):
            r0, r1, r2, r3 = (value[(2 * i + n) * 64 : (2 * i + n) * 64 + 64] for n in range(4))
            rows = slice(i * 64, i * 64 + 64)
            for q, part in enumerate((r0 - r2, r1 - r3, 0.5 * (r1 + r2), 0.5 * (r2 - r1))):
                hi, lo = split(part)
                inner[p, q, rows, 0:384] = hi
                inner[p, q, rows, 384:768] = lo

    signs = (((0, 1),), ((1, -1),), ((0, 1), (1, 1)), ((0, 1), (1, -1)))
    filled = set()
    for p in range(4):
        for q in range(4):
            hi, lo = inner[p, q, :, 0:384], inner[p, q, :, 384:768]
            y = dot(jnp.concatenate([hi, hi], axis=1), weights[p % 2, q])
            y = y + dot(lo, weights[p % 2, q, 0:384, :])
            for j, frame_sign in signs[p]:
                for a, row_sign in signs[q]:
                    term = y if frame_sign * row_sign > 0 else -y
                    acc[j, a] = acc[j, a] + term if (j, a) in filled else term
                    filled.add((j, a))
            if p < 3:
                fill(p + 1, q)

    place = lax.broadcasted_iota(jnp.int32, (64, 1), 0)
    for j in range(2):
        for r in range(6):
            rows = slice((r // 2) * 64, (r // 2) * 64 + 64)
            left = jnp.where(place == 0, 0.0, pltpu.roll(acc[j, r % 2, rows, 0:384], 1, 0))
            right = jnp.where(place == 63, 0.0, pltpu.roll(acc[j, r % 2, rows, 768:1152], 63, 0))
            out = start[j, r * 64 : r * 64 + 64] + b_mid + left + acc[j, r % 2, rows, 384:768] + right
            own_ref[j, r * 64 : r * 64 + 64] = jnp.where(first + 2 + j >= 0, out, 0.0)
    send_ref[...] = own_ref[1 - core]


def upsample_kernel(
    own_ref, got_ref, w_time_ref, b_time_ref, w_up_ref, b_up_ref,
    out_ref,
    hist_hi, hist_lo, x_hi, x_lo, d_hi, d_lo, mixed,
):
    h, s = lax.axis_index("height"), lax.axis_index("seq")
    even_core = lax.rem(s, 2) == 0
    own0, own1, got = own_ref[0], own_ref[1], got_ref[...]
    frames = (
        jnp.where(even_core, own0, got),
        jnp.where(even_core, own1, own0),
        jnp.where(even_core, got, own1),
    )
    for lag, value in enumerate(frames):
        hist_hi[:, lag * 384 : lag * 384 + 384], hist_lo[:, lag * 384 : lag * 384 + 384] = split(value)
    t_hi, t_lo = split(w_time_ref[...])
    paired = dot(hist_hi[...], t_hi) + dot(hist_lo[...], t_hi) + dot(hist_hi[...], t_lo)
    row = lax.broadcasted_iota(jnp.int32, (384, 1), 0) // 64 + (4 * h - 1)
    paired = jnp.where(jnp.logical_and(row >= 0, row < 32), paired + b_time_ref[...][None], 0.0)

    place = lax.broadcasted_iota(jnp.int32, (384, 1), 0) % 64
    for f in range(2):
        x = paired[:, f * 384 : f * 384 + 384]
        left = jnp.where(place == 0, 0.0, pltpu.roll(x, 1, 0))
        right = jnp.where(place == 63, 0.0, pltpu.roll(x, 383, 0))
        for c, value in enumerate((left, x, right)):
            lanes = slice(c * 384, c * 384 + 384)
            x_hi[f, :, lanes], x_lo[f, :, lanes] = split(value[64:320])
            d_hi[f, :, lanes], d_lo[f, :, lanes] = split(value[0:320] - value[64:384])

    b_up = jnp.concatenate([b_up_ref[...][None], jnp.zeros((1, 64), F32)], axis=1)
    for b in range(2):
        weights = []
        for sel in ((0,), (0, 1, 2), (2,)):
            cols = [sum(w_up_ref[r, c] for r in sel) for c in range(3)]
            parts = (cols[0], cols[1] + cols[2]) if b == 0 else (cols[0] + cols[1], cols[2])
            both = jnp.concatenate(parts, axis=1)
            weights.append(split(jnp.concatenate([both, jnp.zeros((64, 768), F32)], axis=0)))
        lanes = slice(b * 384, b * 384 + 768)
        for f in range(2):
            def product(hi, lo, w):
                return dot_lanes(hi, w[0]) + dot_lanes(lo, w[0]) + dot_lanes(hi, w[1])

            m1 = product(d_hi[f, 0:256, lanes], d_lo[f, 0:256, lanes], weights[0])
            m2 = product(x_hi[f, :, lanes], x_lo[f, :, lanes], weights[1]) + b_up
            m3 = product(d_hi[f, 64:320, lanes], d_lo[f, 64:320, lanes], weights[2])
            for a, value in enumerate((m1 + m2, m2 - m3)):
                for i in range(4):
                    for j in range(2):
                        mixed[f, 2 * i + a, j, pl.ds(b, 64, stride=2), :] = value[
                            i * 64 : i * 64 + 64, j * 128 : j * 128 + 128
                        ]
    for f in range(2):
        for p in range(8):
            out_ref[f, p, 0:128, :] = mixed[f, p, 0].T
            out_ref[f, p, 128:192, :] = mixed[f, p, 1].T[0:64]


def pair_kernel(row_ref, other_ref, pair_ref):
    even_core = lax.rem(lax.axis_index("seq"), 2) == 0
    row, other = row_ref[...], other_ref[...]
    pair_ref[...] = jnp.concatenate(
        [jnp.where(even_core, row, other), jnp.where(even_core, other, row)], axis=1
    )


def frames_kernel(slab_ref, before_ref, beside_ref, frames_ref):
    s = lax.axis_index("seq")
    late, even_core = lax.div(s, 2) == 1, lax.rem(s, 2) == 0
    for j in range(2):
        before, beside, slab = before_ref[j], beside_ref[j], slab_ref[j]
        older = jnp.where(even_core, before, beside)[32:64]
        newer = jnp.where(even_core, beside, before)
        frames_ref[j, 0:32] = jnp.where(late, before[0:32], older)
        frames_ref[j, 32:64] = jnp.where(late, before[32:64], newer[0:32])
        frames_ref[j, 64:96] = jnp.where(late, slab[0:32], newer[32:64])
        frames_ref[j, 96:128] = jnp.where(late, slab[32:64], slab[0:32])


def assemble(kernel, shape, *parts):
    return pl.pallas_call(
        kernel,
        out_shape=jax.ShapeDtypeStruct(shape, F32),
        in_specs=[VMEM] * len(parts),
        out_specs=VMEM,
        cost_estimate=pl.CostEstimate(flops=COST, bytes_accessed=1 << 18, transcendentals=0),
        compiler_params=pltpu.CompilerParams(vmem_limit_bytes=2 << 20),
        name="assemble",
    )(*parts)


def gather_latents(latents):
    half = lax.axis_index("seq") // 2
    row = latents[0, :, :, 0, :].reshape(64, 64)
    other = send(row, lambda t, h, s: (t, h, s ^ 1))
    pair = assemble(pair_kernel, (64, 128), row, other)
    other = send(pair, lambda t, h, s: (t, h, s ^ 2))
    slab = jnp.where(half == 0, jnp.stack([pair, other]), jnp.stack([other, pair]))
    before = send(slab, lambda t, h, s: (t + 2 if s == 0 else t + 1, h, s))
    beside = send(before, lambda t, h, s: (t, h, s ^ 1) if s < 2 else None)
    frames = assemble(frames_kernel, (2, 128, 128), slab, before, beside)
    far = send(frames, lambda t, h, s: (t, h + 1 if s % 2 == 0 else h - 1, s))
    near = send(far, lambda t, h, s: (t, h, s ^ 1))
    return frames, far, near


def body(latents, w_in, b_in, norm_gain, norm_shift, w_mid, b_mid, w_time, b_time, w_up, b_up):
    frames, far, near = gather_latents(latents)
    own, outgoing = pl.pallas_call(
        blend_kernel,
        out_shape=(
            jax.ShapeDtypeStruct((2, 384, 384), F32),
            jax.ShapeDtypeStruct((384, 384), F32),
        ),
        in_specs=[VMEM] * 9,
        out_specs=(VMEM, VMEM),
        scratch_shapes=[
            pltpu.VMEM((864, 512), BF16),
            pltpu.VMEM((864, 512), BF16),
            pltpu.VMEM((2, 384, 384), F32),
            pltpu.VMEM((4, 4, 192, 768), BF16),
            pltpu.VMEM((2, 4, 768, 1152), BF16),
            pltpu.VMEM((2, 2, 192, 1152), F32),
        ],
        cost_estimate=pl.CostEstimate(flops=1_000_000, bytes_accessed=1 << 18, transcendentals=0),
        compiler_params=pltpu.CompilerParams(vmem_limit_bytes=36 << 20),
        name="blend",
    )(
        frames, far, near, w_in.reshape(432, 384), b_in, norm_gain, norm_shift, b_mid, w_mid,
    )
    got = send(outgoing, lambda t, h, s: (t, h, s ^ 1))
    out = pl.pallas_call(
        upsample_kernel,
        out_shape=jax.ShapeDtypeStruct((2, 8, 192, 128), F32),
        in_specs=[VMEM] * 6,
        out_specs=VMEM,
        scratch_shapes=[
            pltpu.VMEM((384, 1152), BF16),
            pltpu.VMEM((384, 1152), BF16),
            pltpu.VMEM((2, 256, 1152), BF16),
            pltpu.VMEM((2, 256, 1152), BF16),
            pltpu.VMEM((2, 320, 1152), BF16),
            pltpu.VMEM((2, 320, 1152), BF16),
            pltpu.VMEM((2, 8, 2, 128, 128), F32),
        ],
        compiler_params=pltpu.CompilerParams(vmem_limit_bytes=26 << 20),
        name="upsample",
    )(own, got, w_time.reshape(1152, 768), b_time, jnp.swapaxes(w_up, 2, 3), b_up)
    return jnp.swapaxes(out, 2, 3)[None]


def solution(mesh):
    placed = (P(None, "tm", None, ("height", "seq"), None),) + (P(),) * 10
    return jax.shard_map(
        body,
        mesh=mesh,
        in_specs=placed,
        out_specs=P(None, ("tm", "seq"), "height", None, None),
        check_vma=False,
    )
```

```python
import jax
import jax.numpy as jnp
from jax import lax
from jax.experimental import pallas as pl
from jax.experimental.pallas import tpu as pltpu
from jax.sharding import PartitionSpec as P

EPS = 1e-06
F32 = jnp.float32
BF16 = jnp.bfloat16
AXES = ("tm", "height", "seq")
COST = 10_000_000_000
VMEM = pl.BlockSpec(memory_space=pltpu.VMEM)


def dot_lanes(a, b):
    return lax.dot_general(a, b, (((1,), (1,)), ((), ())), preferred_element_type=F32)


def split(value):
    hi = value.astype(BF16)
    return hi, (value - hi.astype(F32)).astype(BF16)


def dot(a, b):
    return jnp.dot(a, b, preferred_element_type=F32)


def dot_rows(a, b):
    return lax.dot_general(a, b, (((0,), (0,)), ((), ())), preferred_element_type=F32)


def send(value, target):
    n_tm, n_height, n_seq = (lax.axis_size(axis) for axis in AXES)
    place = lambda t, h, s: (t * n_height + h) * n_seq + s
    pairs = []
    for t in range(n_tm):
        for h in range(n_height):
            for s in range(n_seq):
                end = target(t, h, s)
                if end is not None and 0 <= end[0] < n_tm and 0 <= end[1] < n_height:
                    pairs.append((place(t, h, s), place(*end)))
    return lax.ppermute(value, AXES, pairs)


def weights_kernel(raw, weights):
    def rows_of(n, carry):
        hi_rows = pl.ds(pl.multiple_of(n * 16, 16), 16)
        lo_rows = pl.ds(pl.multiple_of(n * 16 + 384, 16), 16)
        for side in range(3):
            for channel in range(0, 384, 128):
                taps = [
                    [raw[lag, down, side, hi_rows, channel : channel + 128] for down in range(3)]
                    for lag in range(3)
                ]
                even = [taps[0][down] + taps[2][down] for down in range(3)]
                over_frames = (
                    taps[0],
                    taps[2],
                    [even[down] + taps[1][down] for down in range(3)],
                    [even[down] - taps[1][down] for down in range(3)],
                )
                lanes = slice(side * 384 + channel, side * 384 + channel + 128)
                for p, (above, at, below) in enumerate(over_frames):
                    outer = above + below
                    for q, w in enumerate((above, below, outer + at, outer - at)):
                        hi, lo = split(w)
                        weights[p, q, hi_rows, lanes] = hi
                        weights[p, q, lo_rows, lanes] = lo
        return carry

    lax.fori_loop(0, 24, rows_of, 0)


def blend_kernel(
    mid_ref, far_ref, near_ref, w_in_ref, b_in_ref, gain_ref, shift_ref, b_mid_ref, weights,
    own_ref, send_ref,
    taps_hi, taps_lo, start, inner, acc,
):
    t, h, s = (lax.axis_index(axis) for axis in AXES)
    core = lax.rem(s, 2)
    first = 4 * t + 2 * lax.div(s, 2) + 2 * core - 4

    mine, far, near = (
        [ref[j, pl.ds(pl.multiple_of(core * 32, 32), 96), :] for j in range(2)]
        for ref in (mid_ref, far_ref, near_ref)
    )
    up = [jnp.where(core == 0, a, b) for a, b in zip(far, near)]
    down = [jnp.where(core == 0, b, a) for a, b in zip(far, near)]
    lat = jnp.concatenate(up + mine + down, axis=1)
    col = lax.broadcasted_iota(jnp.int32, (1, 512), 1) % 64
    for down in range(3):
        for side in range(3):
            offset = 64 * (1 + down) + side - 1
            piece = pltpu.roll(lat, 768 - offset, 1)[:, :512]
            if side == 0:
                piece = jnp.where(col == 0, 0.0, piece)
            if side == 2:
                piece = jnp.where(col == 63, 0.0, piece)
            hi, lo = split(piece)
            for f in range(6):
                at = f * 144 + (down * 3 + side) * 16
                taps_hi[at : at + 16, :] = hi[f * 16 : f * 16 + 16]
                taps_lo[at : at + 16, :] = lo[f * 16 : f * 16 + 16]

    b_in, gain, shift, b_mid = (ref[...][None] for ref in (b_in_ref, gain_ref, shift_ref, b_mid_ref))
    win_hi, win_lo = split(w_in_ref[...])
    row = lax.broadcasted_iota(jnp.int32, (512, 1), 0) // 64 + (4 * h - 2)
    row_ok = jnp.logical_and(row >= 0, row < 32)
    hidden = []
    for f in range(4):
        x_hi = taps_hi[f * 144 : f * 144 + 432, :]
        x_lo = taps_lo[f * 144 : f * 144 + 432, :]
        init = dot_rows(x_hi, win_hi) + dot_rows(x_lo, win_hi) + dot_rows(x_hi, win_lo)
        init = init + b_in
        if f >= 2:
            start[f - 2] = init[64:448]
        mean_square = jnp.mean(init * init, axis=-1, keepdims=True)
        value = init / jnp.sqrt(mean_square + EPS) * gain + shift
        value = value / (1.0 + jnp.exp(-value))
        hidden.append(jnp.where(jnp.logical_and(row_ok, first + f >= 0), value, 0.0))

    d0, d1, d2, d3 = hidden
    for p, value in enumerate((d0 - d2, d1 - d3, 0.5 * (d1 + d2), 0.5 * (d2 - d1))):
        for i in range(3):
            r0, r1, r2, r3 = (value[(2 * i + n) * 64 : (2 * i + n) * 64 + 64] for n in range(4))
            rows = slice(i * 64, i * 64 + 64)
            for q, part in enumerate((r0 - r2, r1 - r3, 0.5 * (r1 + r2), 0.5 * (r2 - r1))):
                hi, lo = split(part)
                inner[p, q, rows, 0:384] = hi
                inner[p, q, rows, 384:768] = lo

    signs = (((0, 1),), ((1, -1),), ((0, 1), (1, 1)), ((0, 1), (1, -1)))
    filled = set()
    for p in range(4):
        for q in range(4):
            hi, lo = inner[p, q, :, 0:384], inner[p, q, :, 384:768]
            y = dot(jnp.concatenate([hi, hi], axis=1), weights[p, q])
            y = y + dot(lo, weights[p, q, 0:384, :])
            for j, frame_sign in signs[p]:
                for a, row_sign in signs[q]:
                    term = y if frame_sign * row_sign > 0 else -y
                    acc[j, a] = acc[j, a] + term if (j, a) in filled else term
                    filled.add((j, a))

    place = lax.broadcasted_iota(jnp.int32, (64, 1), 0)
    for j in range(2):
        for r in range(6):
            rows = slice((r // 2) * 64, (r // 2) * 64 + 64)
            left = jnp.where(place == 0, 0.0, pltpu.roll(acc[j, r % 2, rows, 0:384], 1, 0))
            right = jnp.where(place == 63, 0.0, pltpu.roll(acc[j, r % 2, rows, 768:1152], 63, 0))
            out = start[j, r * 64 : r * 64 + 64] + b_mid + left + acc[j, r % 2, rows, 384:768] + right
            own_ref[j, r * 64 : r * 64 + 64] = jnp.where(first + 2 + j >= 0, out, 0.0)
    send_ref[...] = own_ref[1 - core]


def upsample_kernel(
    own_ref, got_ref, w_time_ref, b_time_ref, w_up_ref, b_up_ref,
    out_ref,
    hist_hi, hist_lo, x_hi, x_lo, d_hi, d_lo, mixed,
):
    h, s = lax.axis_index("height"), lax.axis_index("seq")
    even_core = lax.rem(s, 2) == 0
    own0, own1, got = own_ref[0], own_ref[1], got_ref[...]
    frames = (
        jnp.where(even_core, own0, got),
        jnp.where(even_core, own1, own0),
        jnp.where(even_core, got, own1),
    )
    for lag, value in enumerate(frames):
        hist_hi[:, lag * 384 : lag * 384 + 384], hist_lo[:, lag * 384 : lag * 384 + 384] = split(value)
    t_hi, t_lo = split(w_time_ref[...])
    paired = dot(hist_hi[...], t_hi) + dot(hist_lo[...], t_hi) + dot(hist_hi[...], t_lo)
    row = lax.broadcasted_iota(jnp.int32, (384, 1), 0) // 64 + (4 * h - 1)
    paired = jnp.where(jnp.logical_and(row >= 0, row < 32), paired + b_time_ref[...][None], 0.0)

    place = lax.broadcasted_iota(jnp.int32, (384, 1), 0) % 64
    for f in range(2):
        x = paired[:, f * 384 : f * 384 + 384]
        left = jnp.where(place == 0, 0.0, pltpu.roll(x, 1, 0))
        right = jnp.where(place == 63, 0.0, pltpu.roll(x, 383, 0))
        for c, value in enumerate((left, x, right)):
            lanes = slice(c * 384, c * 384 + 384)
            x_hi[f, :, lanes], x_lo[f, :, lanes] = split(value[64:320])
            d_hi[f, :, lanes], d_lo[f, :, lanes] = split(value[0:320] - value[64:384])

    b_up = jnp.concatenate([b_up_ref[...][None], jnp.zeros((1, 64), F32)], axis=1)
    for b in range(2):
        weights = []
        for sel in ((0,), (0, 1, 2), (2,)):
            cols = [sum(w_up_ref[r, c] for r in sel) for c in range(3)]
            parts = (cols[0], cols[1] + cols[2]) if b == 0 else (cols[0] + cols[1], cols[2])
            both = jnp.concatenate(parts, axis=1)
            weights.append(split(jnp.concatenate([both, jnp.zeros((64, 768), F32)], axis=0)))
        lanes = slice(b * 384, b * 384 + 768)
        for f in range(2):
            def product(hi, lo, w):
                return dot_lanes(hi, w[0]) + dot_lanes(lo, w[0]) + dot_lanes(hi, w[1])

            m1 = product(d_hi[f, 0:256, lanes], d_lo[f, 0:256, lanes], weights[0])
            m2 = product(x_hi[f, :, lanes], x_lo[f, :, lanes], weights[1]) + b_up
            m3 = product(d_hi[f, 64:320, lanes], d_lo[f, 64:320, lanes], weights[2])
            for a, value in enumerate((m1 + m2, m2 - m3)):
                for i in range(4):
                    for j in range(2):
                        mixed[f, 2 * i + a, j, pl.ds(b, 64, stride=2), :] = value[
                            i * 64 : i * 64 + 64, j * 128 : j * 128 + 128
                        ]
    for f in range(2):
        for p in range(8):
            out_ref[f, p, 0:128, :] = mixed[f, p, 0].T
            out_ref[f, p, 128:192, :] = mixed[f, p, 1].T[0:64]


def pair_kernel(row_ref, other_ref, pair_ref):
    even_core = lax.rem(lax.axis_index("seq"), 2) == 0
    row, other = row_ref[...], other_ref[...]
    pair_ref[...] = jnp.concatenate(
        [jnp.where(even_core, row, other), jnp.where(even_core, other, row)], axis=1
    )


def frames_kernel(slab_ref, before_ref, beside_ref, frames_ref):
    s = lax.axis_index("seq")
    late, even_core = lax.div(s, 2) == 1, lax.rem(s, 2) == 0
    for j in range(2):
        before, beside, slab = before_ref[j], beside_ref[j], slab_ref[j]
        older = jnp.where(even_core, before, beside)[32:64]
        newer = jnp.where(even_core, beside, before)
        frames_ref[j, 0:32] = jnp.where(late, before[0:32], older)
        frames_ref[j, 32:64] = jnp.where(late, before[32:64], newer[0:32])
        frames_ref[j, 64:96] = jnp.where(late, slab[0:32], newer[32:64])
        frames_ref[j, 96:128] = jnp.where(late, slab[32:64], slab[0:32])


def assemble(kernel, shape, *parts):
    return pl.pallas_call(
        kernel,
        out_shape=jax.ShapeDtypeStruct(shape, F32),
        in_specs=[VMEM] * len(parts),
        out_specs=VMEM,
        cost_estimate=pl.CostEstimate(flops=COST, bytes_accessed=1 << 18, transcendentals=0),
        compiler_params=pltpu.CompilerParams(vmem_limit_bytes=2 << 20),
        name="assemble",
    )(*parts)


def gather_latents(latents):
    half = lax.axis_index("seq") // 2
    row = latents[0, :, :, 0, :].reshape(64, 64)
    other = send(row, lambda t, h, s: (t, h, s ^ 1))
    pair = assemble(pair_kernel, (64, 128), row, other)
    other = send(pair, lambda t, h, s: (t, h, s ^ 2))
    slab = jnp.where(half == 0, jnp.stack([pair, other]), jnp.stack([other, pair]))
    before = send(slab, lambda t, h, s: (t + 2 if s == 0 else t + 1, h, s))
    beside = send(before, lambda t, h, s: (t, h, s ^ 1) if s < 2 else None)
    frames = assemble(frames_kernel, (2, 128, 128), slab, before, beside)
    far = send(frames, lambda t, h, s: (t, h + 1 if s % 2 == 0 else h - 1, s))
    near = send(far, lambda t, h, s: (t, h, s ^ 1))
    return frames, far, near


def body(latents, w_in, b_in, norm_gain, norm_shift, w_mid, b_mid, w_time, b_time, w_up, b_up):
    frames, far, near = gather_latents(latents)
    weights = pl.pallas_call(
        weights_kernel,
        out_shape=jax.ShapeDtypeStruct((4, 4, 768, 1152), BF16),
        in_specs=[VMEM],
        out_specs=VMEM,
        cost_estimate=pl.CostEstimate(flops=4_000_000_000, bytes_accessed=1 << 18, transcendentals=0),
        compiler_params=pltpu.CompilerParams(vmem_limit_bytes=1 << 20),
        name="weights",
    )(w_mid)
    own, outgoing = pl.pallas_call(
        blend_kernel,
        out_shape=(
            jax.ShapeDtypeStruct((2, 384, 384), F32),
            jax.ShapeDtypeStruct((384, 384), F32),
        ),
        in_specs=[VMEM] * 9,
        out_specs=(VMEM, VMEM),
        scratch_shapes=[
            pltpu.VMEM((864, 512), BF16),
            pltpu.VMEM((864, 512), BF16),
            pltpu.VMEM((2, 384, 384), F32),
            pltpu.VMEM((4, 4, 192, 768), BF16),
            pltpu.VMEM((2, 2, 192, 1152), F32),
        ],
        cost_estimate=pl.CostEstimate(flops=1_000_000, bytes_accessed=1 << 18, transcendentals=0),
        compiler_params=pltpu.CompilerParams(vmem_limit_bytes=24 << 20),
        name="blend",
    )(
        frames, far, near, w_in.reshape(432, 384), b_in, norm_gain, norm_shift, b_mid, weights,
    )
    got = send(outgoing, lambda t, h, s: (t, h, s ^ 1))
    out = pl.pallas_call(
        upsample_kernel,
        out_shape=jax.ShapeDtypeStruct((2, 8, 192, 128), F32),
        in_specs=[VMEM] * 6,
        out_specs=VMEM,
        scratch_shapes=[
            pltpu.VMEM((384, 1152), BF16),
            pltpu.VMEM((384, 1152), BF16),
            pltpu.VMEM((2, 256, 1152), BF16),
            pltpu.VMEM((2, 256, 1152), BF16),
            pltpu.VMEM((2, 320, 1152), BF16),
            pltpu.VMEM((2, 320, 1152), BF16),
            pltpu.VMEM((2, 8, 2, 128, 128), F32),
        ],
        compiler_params=pltpu.CompilerParams(vmem_limit_bytes=24 << 20),
        name="upsample",
    )(own, got, w_time.reshape(1152, 768), b_time, jnp.swapaxes(w_up, 2, 3), b_up)
    return jnp.swapaxes(out, 2, 3)[None]


def solution(mesh):
    placed = (P(None, "tm", None, ("height", "seq"), None),) + (P(),) * 10
    return jax.shard_map(
        body,
        mesh=mesh,
        in_specs=placed,
        out_specs=P(None, ("tm", "seq"), "height", None, None),
        check_vma=False,
    )
```

```python
import jax
import jax.numpy as jnp
from jax import lax
from jax.experimental import pallas as pl
from jax.experimental.pallas import tpu as pltpu
from jax.sharding import PartitionSpec as P

EPS = 1e-06
F32 = jnp.float32
BF16 = jnp.bfloat16
AXES = ("tm", "height", "seq")
COST = 10_000_000_000
VMEM = pl.BlockSpec(memory_space=pltpu.VMEM)


def dot_lanes(a, b):
    return lax.dot_general(a, b, (((1,), (1,)), ((), ())), preferred_element_type=F32)


def split(value):
    hi = value.astype(BF16)
    return hi, (value - hi.astype(F32)).astype(BF16)


def dot(a, b):
    return jnp.dot(a, b, preferred_element_type=F32)


def dot_rows(a, b):
    return lax.dot_general(a, b, (((0,), (0,)), ((), ())), preferred_element_type=F32)


def send(value, target):
    n_tm, n_height, n_seq = (lax.axis_size(axis) for axis in AXES)
    place = lambda t, h, s: (t * n_height + h) * n_seq + s
    pairs = []
    for t in range(n_tm):
        for h in range(n_height):
            for s in range(n_seq):
                end = target(t, h, s)
                if end is not None and 0 <= end[0] < n_tm and 0 <= end[1] < n_height:
                    pairs.append((place(t, h, s), place(*end)))
    return lax.ppermute(value, AXES, pairs)


def weights_kernel(raw, weights):
    def rows_of(n, carry):
        hi_rows = pl.ds(pl.multiple_of(n * 16, 16), 16)
        lo_rows = pl.ds(pl.multiple_of(n * 16 + 384, 16), 16)
        for side in range(3):
            for channel in range(0, 384, 128):
                taps = [
                    [raw[lag, down, side, hi_rows, channel : channel + 128] for down in range(3)]
                    for lag in range(3)
                ]
                even = [taps[0][down] + taps[2][down] for down in range(3)]
                over_frames = (
                    taps[0],
                    taps[2],
                    [even[down] + taps[1][down] for down in range(3)],
                    [even[down] - taps[1][down] for down in range(3)],
                )
                lanes = slice(side * 384 + channel, side * 384 + channel + 128)
                for p, (above, at, below) in enumerate(over_frames):
                    outer = above + below
                    for q, w in enumerate((above, below, outer + at, outer - at)):
                        hi, lo = split(w)
                        weights[p, q, hi_rows, lanes] = hi
                        weights[p, q, lo_rows, lanes] = lo
        return carry

    lax.fori_loop(0, 24, rows_of, 0)


def blend_kernel(
    mid_ref, far_ref, near_ref, w_in_ref, b_in_ref, gain_ref, shift_ref, b_mid_ref, weights,
    own_ref, send_ref,
    taps_hi, taps_lo, start, inner, acc,
):
    t, h, s = (lax.axis_index(axis) for axis in AXES)
    core = lax.rem(s, 2)
    first = 4 * t + 2 * lax.div(s, 2) + 2 * core - 4

    mine, far, near = (
        [ref[j, pl.ds(pl.multiple_of(core * 32, 32), 96), :] for j in range(2)]
        for ref in (mid_ref, far_ref, near_ref)
    )
    up = [jnp.where(core == 0, a, b) for a, b in zip(far, near)]
    down = [jnp.where(core == 0, b, a) for a, b in zip(far, near)]
    lat = jnp.concatenate(up + mine + down, axis=1)
    col = lax.broadcasted_iota(jnp.int32, (1, 512), 1) % 64
    for down in range(3):
        for side in range(3):
            offset = 64 * (1 + down) + side - 1
            piece = pltpu.roll(lat, 768 - offset, 1)[:, :512]
            if side == 0:
                piece = jnp.where(col == 0, 0.0, piece)
            if side == 2:
                piece = jnp.where(col == 63, 0.0, piece)
            hi, lo = split(piece)
            for f in range(6):
                at = f * 144 + (down * 3 + side) * 16
                taps_hi[at : at + 16, :] = hi[f * 16 : f * 16 + 16]
                taps_lo[at : at + 16, :] = lo[f * 16 : f * 16 + 16]

    b_in, gain, shift, b_mid = (ref[...][None] for ref in (b_in_ref, gain_ref, shift_ref, b_mid_ref))
    win_hi, win_lo = split(w_in_ref[...])
    row = lax.broadcasted_iota(jnp.int32, (512, 1), 0) // 64 + (4 * h - 2)
    row_ok = jnp.logical_and(row >= 0, row < 32)
    hidden = []
    for f in range(4):
        x_hi = taps_hi[f * 144 : f * 144 + 432, :]
        x_lo = taps_lo[f * 144 : f * 144 + 432, :]
        init = dot_rows(x_hi, win_hi) + dot_rows(x_lo, win_hi) + dot_rows(x_hi, win_lo)
        init = init + b_in
        if f >= 2:
            start[f - 2] = init[64:448]
        mean_square = jnp.mean(init * init, axis=-1, keepdims=True)
        value = init / jnp.sqrt(mean_square + EPS) * gain + shift
        value = value / (1.0 + jnp.exp(-value))
        hidden.append(jnp.where(jnp.logical_and(row_ok, first + f >= 0), value, 0.0))

    d0, d1, d2, d3 = hidden
    for p, value in enumerate((d0 - d2, d1 - d3, 0.5 * (d1 + d2), 0.5 * (d2 - d1))):
        for i in range(3):
            r0, r1, r2, r3 = (value[(2 * i + n) * 64 : (2 * i + n) * 64 + 64] for n in range(4))
            rows = slice(i * 64, i * 64 + 64)
            for q, part in enumerate((r0 - r2, r1 - r3, 0.5 * (r1 + r2), 0.5 * (r2 - r1))):
                hi, lo = split(part)
                inner[p, q, rows, 0:384] = hi
                inner[p, q, rows, 384:768] = lo

    signs = (((0, 1),), ((1, -1),), ((0, 1), (1, 1)), ((0, 1), (1, -1)))
    filled = set()
    for p in range(4):
        for q in range(4):
            hi, lo = inner[p, q, :, 0:384], inner[p, q, :, 384:768]
            y = dot(jnp.concatenate([hi, hi], axis=1), weights[p, q])
            y = y + dot(lo, weights[p, q, 0:384, :])
            for j, frame_sign in signs[p]:
                for a, row_sign in signs[q]:
                    term = y if frame_sign * row_sign > 0 else -y
                    acc[j, a] = acc[j, a] + term if (j, a) in filled else term
                    filled.add((j, a))

    place = lax.broadcasted_iota(jnp.int32, (64, 1), 0)
    for j in range(2):
        for r in range(6):
            rows = slice((r // 2) * 64, (r // 2) * 64 + 64)
            left = jnp.where(place == 0, 0.0, pltpu.roll(acc[j, r % 2, rows, 0:384], 1, 0))
            right = jnp.where(place == 63, 0.0, pltpu.roll(acc[j, r % 2, rows, 768:1152], 63, 0))
            out = start[j, r * 64 : r * 64 + 64] + b_mid + left + acc[j, r % 2, rows, 384:768] + right
            own_ref[j, r * 64 : r * 64 + 64] = jnp.where(first + 2 + j >= 0, out, 0.0)
    send_ref[...] = own_ref[1 - core]


def upsample_kernel(
    own_ref, got_ref, w_time_ref, b_time_ref, w_up_ref, b_up_ref,
    out_ref,
    hist_hi, hist_lo, x_hi, x_lo, d_hi, d_lo, mixed,
):
    h, s = lax.axis_index("height"), lax.axis_index("seq")
    even_core = lax.rem(s, 2) == 0
    own0, own1, got = own_ref[0], own_ref[1], got_ref[...]
    frames = (
        jnp.where(even_core, own0, got),
        jnp.where(even_core, own1, own0),
        jnp.where(even_core, got, own1),
    )
    for lag, value in enumerate(frames):
        hist_hi[:, lag * 384 : lag * 384 + 384], hist_lo[:, lag * 384 : lag * 384 + 384] = split(value)
    t_hi, t_lo = split(w_time_ref[...])
    paired = dot(hist_hi[...], t_hi) + dot(hist_lo[...], t_hi) + dot(hist_hi[...], t_lo)
    row = lax.broadcasted_iota(jnp.int32, (384, 1), 0) // 64 + (4 * h - 1)
    paired = jnp.where(jnp.logical_and(row >= 0, row < 32), paired + b_time_ref[...][None], 0.0)

    place = lax.broadcasted_iota(jnp.int32, (384, 1), 0) % 64
    for f in range(2):
        x = paired[:, f * 384 : f * 384 + 384]
        left = jnp.where(place == 0, 0.0, pltpu.roll(x, 1, 0))
        right = jnp.where(place == 63, 0.0, pltpu.roll(x, 383, 0))
        for c, value in enumerate((left, x, right)):
            lanes = slice(c * 384, c * 384 + 384)
            x_hi[f, :, lanes], x_lo[f, :, lanes] = split(value[64:320])
            d_hi[f, :, lanes], d_lo[f, :, lanes] = split(value[0:320] - value[64:384])

    b_up = jnp.concatenate([b_up_ref[...][None], jnp.zeros((1, 64), F32)], axis=1)
    for b in range(2):
        weights = []
        for sel in ((0,), (0, 1, 2), (2,)):
            cols = [sum(w_up_ref[r, c] for r in sel) for c in range(3)]
            parts = (cols[0], cols[1] + cols[2]) if b == 0 else (cols[0] + cols[1], cols[2])
            both = jnp.concatenate(parts, axis=1)
            weights.append(split(jnp.concatenate([both, jnp.zeros((64, 768), F32)], axis=0)))
        lanes = slice(b * 384, b * 384 + 768)
        for f in range(2):
            def product(hi, lo, w):
                return dot_lanes(hi, w[0]) + dot_lanes(lo, w[0]) + dot_lanes(hi, w[1])

            m1 = product(d_hi[f, 0:256, lanes], d_lo[f, 0:256, lanes], weights[0])
            m2 = product(x_hi[f, :, lanes], x_lo[f, :, lanes], weights[1]) + b_up
            m3 = product(d_hi[f, 64:320, lanes], d_lo[f, 64:320, lanes], weights[2])
            for a, value in enumerate((m1 + m2, m2 - m3)):
                for i in range(4):
                    for j in range(2):
                        mixed[f, 2 * i + a, j, pl.ds(b, 64, stride=2), :] = value[
                            i * 64 : i * 64 + 64, j * 128 : j * 128 + 128
                        ]
    for f in range(2):
        for p in range(8):
            out_ref[f, p, 0:128, :] = mixed[f, p, 0].T
            out_ref[f, p, 128:192, :] = mixed[f, p, 1].T[0:64]


def pair_kernel(row_ref, other_ref, pair_ref):
    even_core = lax.rem(lax.axis_index("seq"), 2) == 0
    row, other = row_ref[...], other_ref[...]
    pair_ref[...] = jnp.concatenate(
        [jnp.where(even_core, row, other), jnp.where(even_core, other, row)], axis=1
    )


def frames_kernel(slab_ref, before_ref, beside_ref, frames_ref):
    s = lax.axis_index("seq")
    late, even_core = lax.div(s, 2) == 1, lax.rem(s, 2) == 0
    for j in range(2):
        before, beside, slab = before_ref[j], beside_ref[j], slab_ref[j]
        older = jnp.where(even_core, before, beside)[32:64]
        newer = jnp.where(even_core, beside, before)
        frames_ref[j, 0:32] = jnp.where(late, before[0:32], older)
        frames_ref[j, 32:64] = jnp.where(late, before[32:64], newer[0:32])
        frames_ref[j, 64:96] = jnp.where(late, slab[0:32], newer[32:64])
        frames_ref[j, 96:128] = jnp.where(late, slab[32:64], slab[0:32])


def assemble(kernel, shape, *parts):
    return pl.pallas_call(
        kernel,
        out_shape=jax.ShapeDtypeStruct(shape, F32),
        in_specs=[VMEM] * len(parts),
        out_specs=VMEM,
        cost_estimate=pl.CostEstimate(flops=COST, bytes_accessed=1 << 18, transcendentals=0),
        compiler_params=pltpu.CompilerParams(vmem_limit_bytes=2 << 20),
        name="assemble",
    )(*parts)


def gather_latents(latents, w_mid):
    half = lax.axis_index("seq") // 2
    row = latents[0, :, :, 0, :].reshape(64, 64)
    other = send(row, lambda t, h, s: (t, h, s ^ 1))
    pair = assemble(pair_kernel, (64, 128), row, other)
    other = send(pair, lambda t, h, s: (t, h, s ^ 2))
    slab = jnp.where(half == 0, jnp.stack([pair, other]), jnp.stack([other, pair]))
    before = send(slab, lambda t, h, s: (t + 2 if s == 0 else t + 1, h, s))
    beside = send(before, lambda t, h, s: (t, h, s ^ 1) if s < 2 else None)
    frames = assemble(frames_kernel, (2, 128, 128), slab, before, beside)
    far = send(frames, lambda t, h, s: (t, h + 1 if s % 2 == 0 else h - 1, s))
    weights = pl.pallas_call(
        weights_kernel,
        out_shape=jax.ShapeDtypeStruct((4, 4, 768, 1152), BF16),
        in_specs=[VMEM],
        out_specs=VMEM,
        cost_estimate=pl.CostEstimate(flops=4_000_000_000, bytes_accessed=1 << 18, transcendentals=0),
        compiler_params=pltpu.CompilerParams(vmem_limit_bytes=1 << 20),
        name="weights",
    )(w_mid)
    far, weights = lax.optimization_barrier((far, weights))
    near = send(far, lambda t, h, s: (t, h, s ^ 1))
    return frames, far, near, weights


def body(latents, w_in, b_in, norm_gain, norm_shift, w_mid, b_mid, w_time, b_time, w_up, b_up):
    frames, far, near, weights = gather_latents(latents, w_mid)
    own, outgoing = pl.pallas_call(
        blend_kernel,
        out_shape=(
            jax.ShapeDtypeStruct((2, 384, 384), F32),
            jax.ShapeDtypeStruct((384, 384), F32),
        ),
        in_specs=[VMEM] * 9,
        out_specs=(VMEM, VMEM),
        scratch_shapes=[
            pltpu.VMEM((864, 512), BF16),
            pltpu.VMEM((864, 512), BF16),
            pltpu.VMEM((2, 384, 384), F32),
            pltpu.VMEM((4, 4, 192, 768), BF16),
            pltpu.VMEM((2, 2, 192, 1152), F32),
        ],
        cost_estimate=pl.CostEstimate(flops=1_000_000, bytes_accessed=1 << 18, transcendentals=0),
        compiler_params=pltpu.CompilerParams(vmem_limit_bytes=24 << 20),
        name="blend",
    )(
        frames, far, near, w_in.reshape(432, 384), b_in, norm_gain, norm_shift, b_mid, weights,
    )
    got = send(outgoing, lambda t, h, s: (t, h, s ^ 1))
    out = pl.pallas_call(
        upsample_kernel,
        out_shape=jax.ShapeDtypeStruct((2, 8, 192, 128), F32),
        in_specs=[VMEM] * 6,
        out_specs=VMEM,
        scratch_shapes=[
            pltpu.VMEM((384, 1152), BF16),
            pltpu.VMEM((384, 1152), BF16),
            pltpu.VMEM((2, 256, 1152), BF16),
            pltpu.VMEM((2, 256, 1152), BF16),
            pltpu.VMEM((2, 320, 1152), BF16),
            pltpu.VMEM((2, 320, 1152), BF16),
            pltpu.VMEM((2, 8, 2, 128, 128), F32),
        ],
        compiler_params=pltpu.CompilerParams(vmem_limit_bytes=24 << 20),
        name="upsample",
    )(own, got, w_time.reshape(1152, 768), b_time, jnp.swapaxes(w_up, 2, 3), b_up)
    return jnp.swapaxes(out, 2, 3)[None]


def solution(mesh):
    placed = (P(None, "tm", None, ("height", "seq"), None),) + (P(),) * 10
    return jax.shard_map(
        body,
        mesh=mesh,
        in_specs=placed,
        out_specs=P(None, ("tm", "seq"), "height", None, None),
        check_vma=False,
    )
```
